512 devices in a mesh: row: 32 (over z, core), col: 16 (over x, y).
Axes of the slice: x: 4, y: 4, z: 16, core: 2. Of those that a mesh axis runs over, the one named last changes fastest.
Arguments:
- covariance: float32 [2, 4096, 4, 2048], P(None, 'row', None, 'col'), may hold values from 0 to 3, as said below
Outputs:
- factored: float32 [2, 4096, 4, 2048], P(None, 'row', None, 'col')
The draws below stay inside these ranges and needn't reach their ends.
Inputs may be any that keep to these rules, and one draw needn't show every extreme that they name: `covariance`: the matrix of order 8192 is symmetric positive definite; its diagonal entries lie in 1.5 to 3 and the others in 0 to 1.
All inputs are finite; a program needn't handle non-finite values.
Results may differ from the reference program's by a relative error of at most 0.00018.
Values sent between devices are 32-bit elements; how exact they have to be, the bound alone decides.
No kernel may reach another device: no remote copies, remote signals or barrier semaphores. Data moves between devices by JAX's collectives and lax.ppermute only.
A program may use at most 64 MiB of HBM per device.

```python
import jax
import jax.numpy as jnp
from jax import lax

NB = 128
TR = 2
N_ROW = 32
N_COL = 16


def draw_covariance(key, part):
    key = jax.random.fold_in(key, 5)
    key_points, key_nugget = jax.random.split(key, 2)
    total = TR * N_ROW * NB
    points = jax.random.uniform(key_points, (2, total), jnp.float32)
    length_scale = 0.1
    nugget = jnp.exp(jax.random.uniform(key_nugget, (total,), jnp.float32, jnp.log(0.5), jnp.log(2.0)))
    delta_x = points[0][:, None] - points[0][None, :]
    delta_y = points[1][:, None] - points[1][None, :]
    distance = jnp.sqrt(delta_x * delta_x + delta_y * delta_y)
    kernel = jnp.exp(-distance / length_scale)
    same = lax.broadcasted_iota(jnp.int32, (total, total), 0) == lax.broadcasted_iota(jnp.int32, (total, total), 1)
    matrix = jnp.where(same, 1.0 + nugget[:, None], kernel)
    return matrix.astype(jnp.float32).reshape(TR, N_ROW * NB, total // (N_COL * NB), N_COL * NB)


def setup_inputs(seed: int = 0) -> dict:
    arg_keys = jax.random.split(jax.random.key(seed), 2)
    covariance = draw_covariance(jax.random.fold_in(arg_keys[1], 71), 0)
    return dict(covariance=covariance)


def reference(covariance):
    total = covariance.shape[0] * covariance.shape[1]
    matrix = covariance.reshape(total, total)
    for index in range(2):
        start = index * NB
        finish = start + NB
        lower_tile = jnp.linalg.cholesky(matrix[start:finish, start:finish])
        below = jax.scipy.linalg.solve_triangular(lower_tile, matrix[finish:, start:finish].T, lower=True).T
        matrix = matrix.at[finish:, finish:].add(-jnp.dot(below, below.T, precision=lax.Precision.HIGHEST))
        matrix = matrix.at[start:finish, start:finish].set(lower_tile)
        matrix = matrix.at[finish:, start:finish].set(below)
        matrix = matrix.at[start:finish, finish:].set(jnp.float32(0.0))
    return matrix.reshape(covariance.shape)
```

```python
import jax
import jax.numpy as jnp
from jax import lax
from jax.experimental import pallas as pl
from jax.experimental.pallas import tpu as pltpu
from jax.sharding import PartitionSpec as P

NB = 128
ROWS = 32
COLS = 16
F32 = jnp.float32
VMEM = pl.BlockSpec(memory_space=pltpu.VMEM)
SMEM = pl.BlockSpec(memory_space=pltpu.SMEM)


def dot(a, b, dims):
    return lax.dot_general(
        a, b, (dims, ((), ())), precision=lax.Precision.HIGHEST, preferred_element_type=F32
    )


def move(value, pairs):
    flat = [(sp * COLS + sq, dp * COLS + dq) for (sp, sq), (dp, dq) in pairs]
    return lax.ppermute(value, ("row", "col"), flat)


def eliminate(s_ref, e_ref, u_ref, w_ref):
    sub = lax.broadcasted_iota(jnp.int32, (8, NB), 0)

    def spread(x, j):
        return jnp.broadcast_to(x[j : j + 1, :], (8, NB))

    def splat(x, j):
        return jnp.broadcast_to(x[:, j : j + 1], (8, NB))

    def total(terms):
        while len(terms) > 1:
            terms = [terms[i] + terms[i + 1] for i in range(0, len(terms), 2)]
        return terms[0]

    for k in range(NB // 8):
        here = slice(8 * k, 8 * k + 8)
        s = s_ref[here, :]
        e = e_ref[here, :]
        v = [splat(s, 8 * k + j) for j in range(8)]
        for t in range(8):
            pivot = spread(v[t], t)
            inverse = 1.0 / pivot
            root = lax.rsqrt(pivot)
            me = sub == t
            factor = v[t] * inverse

            def step(x):
                row = spread(x, t)
                return row, jnp.where(me, row * inverse, x - factor * row)

            for j in range(t + 1, 8):
                _, v[j] = step(v[j])
            s_row, s = step(s)
            e_row, e = step(e)
            at = 8 * k + t
            u_ref[at : at + 1, :] = (s_row * root)[:1]
            w_ref[at : at + 1, :] = (e_row * root)[:1]
        zs = [spread(s, j) for j in range(8)]
        ze = [spread(e, j) for j in range(8)]
        for h in range(k + 1, NB // 8):
            there = slice(8 * h, 8 * h + 8)
            x = s_ref[there, :]
            y = e_ref[there, :]
            c = [splat(x, 8 * k + j) for j in range(8)]
            s_ref[there, :] = x - total([c[j] * zs[j] for j in range(8)])
            e_ref[there, :] = y - total([c[j] * ze[j] for j in range(8)])


def identity():
    i = lax.broadcasted_iota(jnp.int32, (NB, NB), 0)
    j = lax.broadcasted_iota(jnp.int32, (NB, NB), 1)
    return i, j, jnp.where(i == j, 1.0, 0.0).astype(F32)


def pick_body(place, x, tile, rows, cols):
    first = x[pl.ds(0, NB, stride=4), :]
    odd = (place[0] & 1) == 1
    tile[...] = jnp.where(odd, first.T, first)
    rows[0:NB, :] = first
    rows[NB:, :] = x[pl.ds(4 * NB, NB, stride=4), :]
    for m in range(4):
        cols[NB * m : NB * (m + 1), :] = x[pl.ds(m, NB, stride=4), :]


def factor_body(place, mine, other, u0, w0, m10, u1, w1, s, e):
    even = (place[0] & 1) == 0
    d00 = jnp.where(even, mine[0:NB, :], other[0:NB, :])
    d11 = jnp.where(even, other[0:NB, :], mine[0:NB, :])
    top = jnp.where(even, mine[NB:, :], other[NB:, :])
    bottom = jnp.where(even, other[NB:, :], mine[NB:, :])
    i, j, eye = identity()
    s[...] = d00
    e[...] = eye
    eliminate(s, e, u0, w0)
    u0[...] = jnp.where(i <= j, u0[...], 0.0)
    d01 = jnp.concatenate([top, bottom], axis=0)
    m = dot(w0[...], d01, ((1,), (0,)))
    m10[...] = m
    s[...] = d11 - dot(m, m, ((0,), (0,)))
    e[...] = eye
    eliminate(s, e, u1, w1)
    u1[...] = jnp.where(i <= j, u1[...], 0.0)


def finish_body(place, x, rows_a, rows_b, cols_a, cols_b, u0, w0, m10, u1, w1, out):
    p = place[0]
    q = place[1]
    even = (p & 1) == 0
    direct = (((q + 1) >> 1) & 1) == 0
    w0v = w0[...]
    w1v = w1[...]
    m = m10[...]
    r0 = jnp.where(direct, rows_a[...], rows_b[...])
    r1 = jnp.where(direct, rows_b[...], rows_a[...])
    y0 = dot(r0, w0v, ((1,), (1,)))
    y1 = dot(r1 - dot(y0, m, ((1,), (0,))), w1v, ((1,), (1,)))
    y = jnp.concatenate([y0, y1], axis=1)
    g0 = u0[...].T
    g1 = u1[...].T
    for t in range(4):
        at = slice(NB * t, NB * (t + 1))
        ca = cols_a[at, :]
        cb = cols_b[at, :]
        c0 = jnp.where(even, ca, cb)
        c1 = jnp.where(even, cb, ca)
        x0 = dot(w0v, c0, ((1,), (0,)))
        x1 = dot(w1v, c1 - dot(m, x0, ((0,), (0,))), ((1,), (0,)))
        xx = jnp.concatenate([x0, x1], axis=0)
        change = dot(y, xx, ((1,), (0,)))
        for l in range(2):
            here = pl.ds(4 * NB * l + t, NB, stride=4)
            rs = slice(NB * l, NB * (l + 1))
            new = x[here, :] - change[rs]
            if t == 0:
                new = jnp.where(q == 0, y0[rs], jnp.where(q == 1, y1[rs], new))
            if l == 0:
                if t == 0:
                    new = jnp.where(
                        p == 0,
                        jnp.where(q == 0, g0, 0.0),
                        jnp.where(
                            p == 1,
                            jnp.where(q == 0, y0[rs], jnp.where(q == 1, g1, 0.0)),
                            new,
                        ),
                    )
                else:
                    new = jnp.where(p < 2, 0.0, new)
            out[here, :] = new


def tile_of(*rows):
    return [jax.ShapeDtypeStruct((r, NB), F32) for r in rows]


def per_device(covariance):
    p = lax.axis_index("row")
    q = lax.axis_index("col")
    z = p >> 1
    x = q >> 2
    y = q & 3
    odd = (p & 1) == 1
    place = jnp.stack([p, q]).astype(jnp.int32)
    local = covariance.reshape(2 * NB * 4, NB)
    tile, rows, cols = pl.pallas_call(
        pick_body,
        out_shape=tile_of(NB, 2 * NB, 4 * NB),
        in_specs=[SMEM, VMEM],
        out_specs=[VMEM] * 3,
    )(place, local)

    cores = (0, 1)
    planes = range(16)
    squares = range(4)

    r1 = move(tile, [((c, a), (c, b)) for c in cores for a, b in ((0, 2), (1, 3))])
    r2 = move(tile, [((c, a), (c, b)) for c in cores for a, b in ((0, 3), (1, 2))])
    r3 = move(tile, [((c, a), (c, b)) for c in cores for a, b in ((0, 1), (1, 0))])
    first = jnp.where(y == 0, tile, jnp.where(y == 1, r3, jnp.where(y == 2, r1, r2)))
    second = jnp.where(y == 0, r3, jnp.where(y == 1, tile, jnp.where(y == 2, r2, r1)))
    diag = jnp.concatenate(
        [
            jnp.where(odd, second, first),
            jnp.where(odd, first[NB // 2 :], second[: NB // 2]),
        ],
        axis=0,
    )
    got = [
        move(diag, [((c, a), (c, 4 * b + a)) for c in cores for a in squares]) for b in (2, 1, 3)
    ]
    diag = jnp.where(x == 0, diag, got[0] + got[1] + got[2])
    got = [
        move(diag, [((c, a), (2 * b + c, a)) for c in cores for a in range(COLS)]) for b in (8, 4, 12)
    ]
    diag = jnp.where(z == 0, diag, got[0] + got[1] + got[2])
    got = [
        move(
            diag,
            [
                ((2 * s + c, a), (2 * (s + b) + c, a))
                for c in cores
                for s in (0, 4, 8, 12)
                for a in range(COLS)
            ],
        )
        for b in (2, 1, 3)
    ]
    diag = jnp.where((z & 3) == 0, diag, got[0] + got[1] + got[2])
    swap = [((r, a), (r ^ 1, a)) for r in range(ROWS) for a in range(COLS)]
    other = move(diag, swap)

    got = move(rows, [((r, a), (r, b)) for r in range(ROWS) for a, b in ((0, 3), (1, 2))])
    rows = jnp.where(y >= 2, got, rows)
    got = move(rows, [((r, a), (r, 8 + a)) for r in range(ROWS) for a in squares])
    rows = jnp.where(x == 2, got, rows)
    got = move(
        rows, [((r, 4 * b + a), (r, 4 * b + 4 + a)) for r in range(ROWS) for b in (0, 2) for a in squares]
    )
    rows = jnp.where((x & 1) == 1, got, rows)
    rows_b = move(
        rows, [((r, a), (r, a ^ 1)) for r in range(ROWS) for a in range(COLS)]
    )

    for stride in (8, 4, 2, 1):
        pairs = []
        for s in range(0, 16, 2 * stride):
            for c in cores:
                d = (s + stride if c == 0 else s - stride) % 16
                pairs += [((2 * s + c, a), (2 * d + c, a)) for a in range(COLS)]
        got = move(cols, pairs)
        cols = jnp.where((z & (2 * stride - 1)) == stride, got, cols)
    cols_b = move(cols, swap)

    factors = pl.pallas_call(
        factor_body,
        out_shape=tile_of(*([NB] * 5)),
        in_specs=[SMEM, VMEM, VMEM],
        out_specs=[VMEM] * 5,
        scratch_shapes=[pltpu.VMEM((NB, NB), F32)] * 2,
        cost_estimate=pl.CostEstimate(flops=10_000_000, bytes_accessed=400_000, transcendentals=0),
    )(place, diag, other)
    out = pl.pallas_call(
        finish_body,
        out_shape=jax.ShapeDtypeStruct((2 * NB * 4, NB), F32),
        in_specs=[SMEM] + [VMEM] * 10,
        out_specs=VMEM,
    )(place, local, rows, rows_b, cols, cols_b, *factors)
    return out.reshape(covariance.shape)


def solution(mesh):
    spec = P(None, "row", None, "col")
    return jax.shard_map(
        per_device, mesh=mesh, in_specs=(spec,), out_specs=spec, check_vma=False
    )
```

```python
import jax
import jax.numpy as jnp
from jax import lax
from jax.experimental import pallas as pl
from jax.experimental.pallas import tpu as pltpu
from jax.sharding import PartitionSpec as P

NB = 128
ROWS = 32
COLS = 16
F32 = jnp.float32
VMEM = pl.BlockSpec(memory_space=pltpu.VMEM)
PARAMS = pltpu.CompilerParams(vmem_limit_bytes=8 * 2**20)


def dot(a, b, dims):
    return lax.dot_general(
        a, b, (dims, ((), ())), precision=lax.Precision.HIGHEST, preferred_element_type=F32
    )


def move(value, pairs):
    flat = [(sp * COLS + sq, dp * COLS + dq) for (sp, sq), (dp, dq) in pairs]
    return lax.ppermute(value, ("row", "col"), flat)


def after(value, earlier):
    return lax.optimization_barrier((value, earlier))[0]


def eliminate(s_ref, e_ref, u_ref, w_ref):
    sub = lax.broadcasted_iota(jnp.int32, (8, NB), 0)

    def spread(x, j):
        return jnp.broadcast_to(x[j : j + 1, :], (8, NB))

    def splat(x, j):
        return jnp.broadcast_to(x[:, j : j + 1], (8, NB))

    def total(terms):
        while len(terms) > 1:
            terms = [terms[i] + terms[i + 1] for i in range(0, len(terms), 2)]
        return terms[0]

    for k in range(NB // 8):
        here = slice(8 * k, 8 * k + 8)
        s = s_ref[here, :]
        e = e_ref[here, :]
        v = [splat(s, 8 * k + j) for j in range(8)]
        for t in range(8):
            pivot = spread(v[t], t)
            inverse = 1.0 / pivot
            root = lax.rsqrt(pivot)
            me = sub == t
            factor = v[t] * inverse

            def step(x):
                row = spread(x, t)
                return row, jnp.where(me, row * inverse, x - factor * row)

            for j in range(t + 1, 8):
                _, v[j] = step(v[j])
            s_row, s = step(s)
            e_row, e = step(e)
            at = 8 * k + t
            u_ref[at : at + 1, :] = (s_row * root)[:1]
            w_ref[at : at + 1, :] = (e_row * root)[:1]
        zs = [spread(s, j) for j in range(8)]
        ze = [spread(e, j) for j in range(8)]
        for h in range(k + 1, NB // 8):
            there = slice(8 * h, 8 * h + 8)
            x = s_ref[there, :]
            y = e_ref[there, :]
            c = [splat(x, 8 * k + j) for j in range(8)]
            s_ref[there, :] = x - total([c[j] * zs[j] for j in range(8)])
            e_ref[there, :] = y - total([c[j] * ze[j] for j in range(8)])


def identity():
    i = lax.broadcasted_iota(jnp.int32, (NB, NB), 0)
    j = lax.broadcasted_iota(jnp.int32, (NB, NB), 1)
    return i, j, jnp.where(i == j, 1.0, 0.0).astype(F32)


def pick_body(x, tile, rows, cols):
    first = x[pl.ds(0, NB, stride=4), :]
    odd = (lax.axis_index("row") & 1) == 1
    tile[...] = jnp.where(odd, first.T, first)
    rows[0:NB, :] = first
    rows[NB:, :] = x[pl.ds(4 * NB, NB, stride=4), :]
    for m in range(4):
        cols[NB * m : NB * (m + 1), :] = x[pl.ds(m, NB, stride=4), :]


def first_body(mine, other, u0, w0, m10, s11, s, e):
    even = (lax.axis_index("row") & 1) == 0
    d00 = jnp.where(even, mine[0:NB, :], other[0:NB, :])
    d11 = jnp.where(even, other[0:NB, :], mine[0:NB, :])
    top = jnp.where(even, mine[NB:, :], other[NB:, :])
    bottom = jnp.where(even, other[NB:, :], mine[NB:, :])
    i, j, eye = identity()
    s[...] = d00
    e[...] = eye
    eliminate(s, e, u0, w0)
    u0[...] = jnp.where(i <= j, u0[...], 0.0)
    d01 = jnp.concatenate([top, bottom], axis=0)
    m = dot(w0[...], d01, ((1,), (0,)))
    m10[...] = m
    s11[...] = d11 - dot(m, m, ((0,), (0,)))


def second_body(s11, u1, w1, s, e):
    i, j, eye = identity()
    s[...] = s11[...]
    e[...] = eye
    eliminate(s, e, u1, w1)
    u1[...] = jnp.where(i <= j, u1[...], 0.0)


def finish_body(x, rows_a, rows_b, cols_a, cols_b, u0, w0, m10, u1, w1, out):
    p = lax.axis_index("row")
    q = lax.axis_index("col")
    even = (p & 1) == 0
    direct = (((q + 1) >> 1) & 1) == 0
    w0v = w0[...]
    w1v = w1[...]
    m = m10[...]
    r0 = jnp.where(direct, rows_a[...], rows_b[...])
    r1 = jnp.where(direct, rows_b[...], rows_a[...])
    y0 = dot(r0, w0v, ((1,), (1,)))
    y1 = dot(r1 - dot(y0, m, ((1,), (0,))), w1v, ((1,), (1,)))
    y = jnp.concatenate([y0, y1], axis=1)
    g0 = u0[...].T
    g1 = u1[...].T
    for t in range(4):
        at = slice(NB * t, NB * (t + 1))
        ca = cols_a[at, :]
        cb = cols_b[at, :]
        c0 = jnp.where(even, ca, cb)
        c1 = jnp.where(even, cb, ca)
        x0 = dot(w0v, c0, ((1,), (0,)))
        x1 = dot(w1v, c1 - dot(m, x0, ((0,), (0,))), ((1,), (0,)))
        xx = jnp.concatenate([x0, x1], axis=0)
        change = dot(y, xx, ((1,), (0,)))
        for l in range(2):
            here = pl.ds(4 * NB * l + t, NB, stride=4)
            rs = slice(NB * l, NB * (l + 1))
            new = x[here, :] - change[rs]
            if t == 0:
                new = jnp.where(q == 0, y0[rs], jnp.where(q == 1, y1[rs], new))
            if l == 0:
                if t == 0:
                    new = jnp.where(
                        p == 0,
                        jnp.where(q == 0, g0, 0.0),
                        jnp.where(
                            p == 1,
                            jnp.where(q == 0, y0[rs], jnp.where(q == 1, g1, 0.0)),
                            new,
                        ),
                    )
                else:
                    new = jnp.where(p < 2, 0.0, new)
            out[here, :] = new


def tile_of(*rows):
    return [jax.ShapeDtypeStruct((r, NB), F32) for r in rows]


def call(body, shapes, scratch, *args):
    return pl.pallas_call(
        body,
        out_shape=shapes,
        in_specs=[VMEM] * len(args),
        out_specs=[VMEM] * len(shapes),
        scratch_shapes=[pltpu.VMEM((NB, NB), F32)] * scratch,
        compiler_params=PARAMS,
    )(*args)


def per_device(covariance):
    p = lax.axis_index("row")
    q = lax.axis_index("col")
    z = p >> 1
    x = q >> 2
    y = q & 3
    odd = (p & 1) == 1
    local = covariance.reshape(2 * NB * 4, NB)
    tile, rows, cols = call(pick_body, tile_of(NB, 2 * NB, 4 * NB), 0, local)

    cores = (0, 1)
    every = range(COLS)
    squares = range(4)
    swap = [((r, a), (r ^ 1, a)) for r in range(ROWS) for a in every]

    def climb(cols, stride):
        pairs = []
        for s in range(0, 16, 2 * stride):
            for c in cores:
                d = (s + stride if c == 0 else s - stride) % 16
                pairs += [((2 * s + c, a), (2 * d + c, a)) for a in every]
        got = move(cols, pairs)
        return jnp.where((z & (2 * stride - 1)) == stride, got, cols)

    r1 = move(tile, [((c, a), (c, b)) for c in cores for a, b in ((0, 2), (1, 3))])
    r2 = move(tile, [((c, a), (c, b)) for c in cores for a, b in ((0, 3), (1, 2))])
    r3 = move(tile, [((c, a), (c, b)) for c in cores for a, b in ((0, 1), (1, 0))])
    first = jnp.where(y == 0, tile, jnp.where(y == 1, r3, jnp.where(y == 2, r1, r2)))
    second = jnp.where(y == 0, r3, jnp.where(y == 1, tile, jnp.where(y == 2, r2, r1)))
    diag = jnp.concatenate(
        [
            jnp.where(odd, second, first),
            jnp.where(odd, first[NB // 2 :], second[: NB // 2]),
        ],
        axis=0,
    )
    got = move(rows, [((r, a), (r, b)) for r in range(ROWS) for a, b in ((0, 3), (1, 2))])
    rows = jnp.where(y >= 2, got, rows)

    got = [
        move(diag, [((c, a), (c, 4 * b + a)) for c in cores for a in squares]) for b in (2, 1, 3)
    ]
    cols = climb(after(cols, diag), 8)
    rows = after(rows, diag)
    rows_got = move(rows, [((r, a), (r, 8 + a)) for r in range(ROWS) for a in squares])
    diag = jnp.where(x == 0, diag, got[0] + got[1] + got[2])
    rows = jnp.where(x == 2, rows_got, rows)

    got = [
        move(diag, [((c, a), (2 * b + c, a)) for c in cores for a in every]) for b in (8, 4, 12)
    ]
    cols = climb(after(cols, diag), 4)
    rows = after(rows, diag)
    rows_got = move(
        rows, [((r, 4 * b + a), (r, 4 * b + 4 + a)) for r in range(ROWS) for b in (0, 2) for a in squares]
    )
    diag = jnp.where(z == 0, diag, got[0] + got[1] + got[2])
    rows = jnp.where((x & 1) == 1, rows_got, rows)

    got = [
        move(
            diag,
            [
                ((2 * s + c, a), (2 * (s + b) + c, a))
                for c in cores
                for s in (0, 4, 8, 12)
                for a in every
            ],
        )
        for b in (2, 1, 3)
    ]
    cols = climb(after(cols, diag), 2)
    diag = jnp.where((z & 3) == 0, diag, got[0] + got[1] + got[2])

    other = move(diag, swap)
    cols = climb(after(cols, diag), 1)
    rows_b = move(after(rows, diag), [((r, a), (r, a ^ 1)) for r in range(ROWS) for a in every])

    u0, w0, m10, s11 = call(first_body, tile_of(*[NB] * 4), 2, diag, other)
    cols_b = move(after(cols, s11), swap)
    u1, w1 = call(second_body, tile_of(*[NB] * 2), 2, s11)
    (out,) = call(
        finish_body, tile_of(8 * NB), 0, local, rows, rows_b, cols, cols_b, u0, w0, m10, u1, w1
    )
    return out.reshape(covariance.shape)


def solution(mesh):
    spec = P(None, "row", None, "col")
    return jax.shard_map(
        per_device, mesh=mesh, in_specs=(spec,), out_specs=spec, check_vma=False
    )
```

```python
import jax
import jax.numpy as jnp
from jax import lax
from jax.experimental import pallas as pl
from jax.experimental.pallas import tpu as pltpu
from jax.sharding import PartitionSpec as P

NB = 128
ROWS = 32
COLS = 16
F32 = jnp.float32
VMEM = pl.BlockSpec(memory_space=pltpu.VMEM)
COST = 10**9
PARAMS = pltpu.CompilerParams(vmem_limit_bytes=8 * 2**20)


def dot(a, b, dims):
    return lax.dot_general(
        a, b, (dims, ((), ())), precision=lax.Precision.HIGHEST, preferred_element_type=F32
    )


def move(value, pairs):
    flat = [(sp * COLS + sq, dp * COLS + dq) for (sp, sq), (dp, dq) in pairs]
    return lax.ppermute(value, ("row", "col"), flat)


def after(value, earlier):
    return lax.optimization_barrier((value, earlier))[0]


def invert_factor(x_ref, w_ref):
    sub = lax.broadcasted_iota(jnp.int32, (8, NB), 0)
    lane = lax.broadcasted_iota(jnp.int32, (8, NB), 1)

    def spread(x, j):
        return jnp.broadcast_to(x[j : j + 1, :], (8, NB))

    def splat(x, j):
        return jnp.broadcast_to(x[:, j : j + 1], (8, NB))

    for k in range(NB // 8):
        here = x_ref[8 * k : 8 * k + 8, :]
        v = [splat(here, 8 * k + j) for j in range(8)]
        mine = (lane >= 8 * k) & (lane < 8 * k + 8)
        rest = jnp.where(mine, jnp.where(lane == sub + 8 * k, 1.0, 0.0), here)
        for t in range(0, 8, 2):
            a = spread(v[t], t)
            b = spread(v[t], t + 1)
            c = spread(v[t + 1], t + 1)
            det = a * c - b * b
            scale = 1.0 / det
            i00 = c * scale
            i01 = b * scale
            i11 = a * scale
            f0 = jnp.where(
                sub == t, 1.0 - i00, jnp.where(sub == t + 1, i01, v[t] * i00 - v[t + 1] * i01)
            )
            f1 = jnp.where(
                sub == t, i01, jnp.where(sub == t + 1, 1.0 - i11, v[t + 1] * i11 - v[t] * i01)
            )
            for j in range(t + 2, 8):
                v[j] = v[j] - f0 * spread(v[j], t) - f1 * spread(v[j], t + 1)
            r0 = spread(rest, t)
            r1 = spread(rest, t + 1)
            over = 1.0 / a
            at = 8 * k + t
            w_ref[at : at + 1, :] = (r0 * lax.rsqrt(a))[:1]
            w_ref[at + 1 : at + 2, :] = ((r1 - (b * over) * r0) * lax.rsqrt(det * over))[:1]
            rest = rest - f0 * r0 - f1 * r1
        z = [spread(rest, j) for j in range(8)]
        for h in range(k + 1, NB // 8):
            there = slice(8 * h, 8 * h + 8)
            x = x_ref[there, :]
            terms = [splat(x, 8 * k + j) * z[j] for j in range(8)]
            while len(terms) > 1:
                terms = [terms[i] + terms[i + 1] for i in range(0, len(terms), 2)]
            x_ref[there, :] = jnp.where(mine, 0.0, x) - terms[0]


def indices():
    i = lax.broadcasted_iota(jnp.int32, (NB, NB), 0)
    return i, lax.broadcasted_iota(jnp.int32, (NB, NB), 1)


def pick_body(x, tile, rows, cols):
    first = x[pl.ds(0, NB, stride=4), :]
    odd = (lax.axis_index("row") & 1) == 1
    tile[...] = jnp.where(odd, first.T, first)
    rows[0:NB, :] = first
    rows[NB:, :] = x[pl.ds(4 * NB, NB, stride=4), :]
    for m in range(4):
        cols[NB * m : NB * (m + 1), :] = x[pl.ds(m, NB, stride=4), :]


def token_body(*refs):
    out = refs[-1]
    total = refs[0][...]
    for ref in refs[1:-1]:
        total = total + ref[...]
    out[...] = total


def first_body(mine, other, w0, m10, s11, x):
    even = (lax.axis_index("row") & 1) == 0
    i, j = indices()
    x[...] = jnp.where(even, mine[0:NB, :], other[0:NB, :])
    invert_factor(x, w0)
    w = jnp.where(i >= j, w0[...], 0.0)
    w0[...] = w
    top = jnp.where(even, mine[NB:, :], other[NB:, :])
    bottom = jnp.where(even, other[NB:, :], mine[NB:, :])
    m = dot(w, jnp.concatenate([top, bottom], axis=0), ((1,), (0,)))
    m10[...] = m
    s11[...] = jnp.where(even, other[0:NB, :], mine[0:NB, :]) - dot(m, m, ((0,), (0,)))


def second_body(s11, mark, w1, x):
    i, j = indices()
    x[...] = s11[...]
    invert_factor(x, w1)
    w1[...] = jnp.where(i >= j, w1[...], 0.0)


def finish_body(x, rows_a, rows_b, cols_a, cols_b, w0, m10, w1, out):
    p = lax.axis_index("row")
    q = lax.axis_index("col")
    even = (p & 1) == 0
    direct = (((q + 1) >> 1) & 1) == 0
    i, j = indices()
    low = i >= j
    w0v = w0[...]
    w1v = w1[...]
    m = m10[...]
    r0 = jnp.where(direct, rows_a[...], rows_b[...])
    r1 = jnp.where(direct, rows_b[...], rows_a[...])
    y0 = dot(r0, w0v, ((1,), (1,)))
    y1 = dot(r1 - dot(y0, m, ((1,), (0,))), w1v, ((1,), (1,)))
    y = jnp.concatenate([y0, y1], axis=1)
    for t in range(4):
        at = slice(NB * t, NB * (t + 1))
        ca = cols_a[at, :]
        cb = cols_b[at, :]
        x0 = dot(w0v, jnp.where(even, ca, cb), ((1,), (0,)))
        x1 = dot(w1v, jnp.where(even, cb, ca) - dot(m, x0, ((0,), (0,))), ((1,), (0,)))
        change = dot(y, jnp.concatenate([x0, x1], axis=0), ((1,), (0,)))
        for l in range(2):
            here = pl.ds(4 * NB * l + t, NB, stride=4)
            rs = slice(NB * l, NB * (l + 1))
            new = x[here, :] - change[rs]
            if t == 0:
                panel = jnp.where(q == 0, y0[rs], y1[rs])
                if l == 0:
                    panel = jnp.where((p != q) | low, panel, 0.0)
                    panel = jnp.where((p == 0) & (q == 1), 0.0, panel)
                new = jnp.where(q < 2, panel, new)
                if l == 0:
                    new = jnp.where((p < 2) & (q >= 2), 0.0, new)
            elif l == 0:
                new = jnp.where(p < 2, 0.0, new)
            out[here, :] = new


def tile_of(*rows):
    return [jax.ShapeDtypeStruct((r, NB), F32) for r in rows]


LONG = pl.CostEstimate(flops=COST, bytes_accessed=COST, transcendentals=0)


def call(body, shapes, scratch, *args, cost=None):
    return pl.pallas_call(
        body,
        out_shape=shapes,
        in_specs=[VMEM] * len(args),
        out_specs=[VMEM] * len(shapes),
        scratch_shapes=[pltpu.VMEM((NB, NB), F32)] * scratch,
        compiler_params=PARAMS,
        cost_estimate=cost,
    )(*args)


def token(*xs):
    block = pl.BlockSpec((8, NB), lambda i: (0, 0))
    return pl.pallas_call(
        token_body,
        grid=(1,),
        out_shape=jax.ShapeDtypeStruct((8, NB), F32),
        in_specs=[block] * len(xs),
        out_specs=block,
        compiler_params=PARAMS,
        cost_estimate=LONG,
    )(*xs)


def per_device(covariance):
    p = lax.axis_index("row")
    q = lax.axis_index("col")
    z = p >> 1
    x = q >> 2
    y = q & 3
    odd = (p & 1) == 1
    local = covariance.reshape(2 * NB * 4, NB)
    tile, rows, cols = call(pick_body, tile_of(NB, 2 * NB, 4 * NB), 0, local)

    cores = (0, 1)
    every = range(COLS)
    squares = range(4)
    tied = lax.optimization_barrier

    def in_row(value, pairs):
        return move(value, [((r, a), (r, b)) for r in range(ROWS) for a, b in pairs])

    def along_x(s, d):
        return [(4 * s + a, 4 * d + a) for a in squares]

    def along_z(value, sends, on=cores):
        return move(
            value, [((2 * s + c, a), (2 * d + c, a)) for s, d in sends for c in on for a in every]
        )

    def among(h, members):
        hit = h == members[0]
        for m in members[1:]:
            hit = hit | (h == m)
        return hit

    def take(old, h, got, sends):
        for value, each in zip(got, sends):
            old = jnp.where(among(h, [d for _, d in each]), value, old)
        return old

    swap = [((r, a), (r ^ 1, a)) for r in range(ROWS) for a in every]

    def lift(value, sends):
        return [along_z(value, each) for each in sends]

    r3 = move(tile, [((c, a), (c, b)) for c in cores for a, b in ((0, 1), (1, 0))])
    r1 = move(tile, [((c, a), (c, b)) for c in cores for a, b in ((0, 2), (1, 3))])
    r2 = move(tile, [((c, a), (c, b)) for c in cores for a, b in ((0, 3), (1, 2))])
    for sends in ([(0, 1)], [(1, 5)]):
        cols = take(cols, z, lift(cols, [sends]), [sends])
    c_sends = [[(1, 13), (5, 9)]]
    c_got = lift(cols, c_sends)
    first = jnp.where(y == 0, tile, jnp.where(y == 1, r3, jnp.where(y == 2, r1, r2)))
    second = jnp.where(y == 0, r3, jnp.where(y == 1, tile, jnp.where(y == 2, r2, r1)))
    diag = jnp.concatenate(
        [
            jnp.where(odd, second, first),
            jnp.where(odd, first[NB // 2 :], second[: NB // 2]),
        ],
        axis=0,
    )

    got = [move(diag, [((c, a), (c, b)) for c in cores for a, b in along_x(0, d)]) for d in (2, 1, 3)]
    cols = take(cols, z, c_got, c_sends)
    cols = tied((cols, diag))[0]
    q_sends = [[(1, 2), (5, 4), (13, 12), (9, 8)]]
    q_got = lift(cols, q_sends)
    r_got = in_row(tied((rows, diag))[0], [(0, 3), (1, 2)])
    rows = jnp.where((y >= 2) & (x == 0), r_got, rows)
    far = in_row(tied((rows, diag))[0], along_x(0, 2))
    diag = take(diag, x, got, [[(0, 2)], [(0, 1)], [(0, 3)]])
    diag, mark = tied((diag, token(diag, diag, r_got)))

    d_sends = [[(0, 4)], [(0, 12)], [(0, 2)]]
    got = lift(diag, d_sends)
    rows = jnp.where(x == 2, far, rows)
    r_got = in_row(tied((rows, mark))[0], along_x(0, 1) + along_x(2, 3))
    diag = take(diag, z, got, d_sends)
    diag, mark = tied((diag, token(diag, mark)))

    d_sends = [
        [(0, 13), (2, 5), (4, 8), (12, 9)],
        [(0, 14), (2, 3), (4, 7), (12, 10)],
        [(0, 15), (2, 1), (4, 6), (12, 11)],
    ]
    got = lift(diag, d_sends)
    late_sends = [[(1, 3), (5, 6), (9, 10), (13, 14)], [(5, 7), (9, 11), (13, 15)]]
    late_got = [along_z(tied((cols, mark))[0], each) for each in late_sends]
    diag = take(diag, z, got, d_sends)
    diag, mark = tied((diag, token(diag, mark, *late_got)))

    other = move(diag, swap)
    rows = jnp.where((x & 1) == 1, r_got, rows)
    rows_b = in_row(tied((rows, mark))[0], [(a, a ^ 1) for a in every])
    w0, m10, s11 = call(first_body, tile_of(NB, NB, NB), 1, diag, other)
    cols = take(cols, z, q_got + late_got, q_sends + late_sends)
    cols_b = move(tied((cols, s11))[0], swap)
    (w1,) = call(second_body, tile_of(NB), 1, s11, w0[:8], cost=LONG)
    (out,) = call(
        finish_body, tile_of(8 * NB), 0, local, rows, rows_b, cols, cols_b, w0, m10, w1
    )
    return out.reshape(covariance.shape)


def solution(mesh):
    spec = P(None, "row", None, "col")
    return jax.shard_map(
        per_device, mesh=mesh, in_specs=(spec,), out_specs=spec, check_vma=False
    )
```

```python
import jax
import jax.numpy as jnp
from jax import lax
from jax.experimental import pallas as pl
from jax.experimental.pallas import tpu as pltpu
from jax.sharding import PartitionSpec as P

NB = 128
ROWS = 32
COLS = 16
F32 = jnp.float32
VMEM = pl.BlockSpec(memory_space=pltpu.VMEM)
COST = 10**9
PARAMS = pltpu.CompilerParams(vmem_limit_bytes=8 * 2**20)


def dot(a, b, dims):
    return lax.dot_general(
        a, b, (dims, ((), ())), precision=lax.Precision.HIGHEST, preferred_element_type=F32
    )


def move(value, pairs):
    flat = [(sp * COLS + sq, dp * COLS + dq) for (sp, sq), (dp, dq) in pairs]
    return lax.ppermute(value, ("row", "col"), flat)


def after(value, earlier):
    return lax.optimization_barrier((value, earlier))[0]


def invert_factor(x_ref, w_ref):
    sub = lax.broadcasted_iota(jnp.int32, (8, NB), 0)
    lane = lax.broadcasted_iota(jnp.int32, (8, NB), 1)
    wide = 16
    groups = range(wide // 8)

    def spread(x, j):
        return jnp.broadcast_to(x[j % 8 : j % 8 + 1, :], (8, NB))

    def splat(x, j):
        return jnp.broadcast_to(x[:, j : j + 1], (8, NB))

    for start in range(0, NB, wide):
        here = [x_ref[start + 8 * g : start + 8 * g + 8, :] for g in groups]
        v = [[splat(here[g], start + j) for g in groups] for j in range(wide)]
        mine = (lane >= start) & (lane < start + wide)
        rest = [
            jnp.where(mine, jnp.where(lane == sub + (start + 8 * g), 1.0, 0.0), here[g])
            for g in groups
        ]
        for t in range(0, wide, 2):
            home = t // 8
            u = t % 8
            a = spread(v[t][home], t)
            b = spread(v[t][home], t + 1)
            c = spread(v[t + 1][home], t + 1)
            det = a * c - b * b
            scale = 1.0 / det
            i00 = c * scale
            i01 = b * scale
            i11 = a * scale
            f0 = []
            f1 = []
            for g in groups:
                p0 = v[t][g] * i00 - v[t + 1][g] * i01
                p1 = v[t + 1][g] * i11 - v[t][g] * i01
                if g == home:
                    p0 = jnp.where(sub == u, 1.0 - i00, jnp.where(sub == u + 1, i01, p0))
                    p1 = jnp.where(sub == u, i01, jnp.where(sub == u + 1, 1.0 - i11, p1))
                f0.append(p0)
                f1.append(p1)
            for j in range(t + 2, wide):
                s0 = spread(v[j][home], t)
                s1 = spread(v[j][home], t + 1)
                v[j] = [v[j][g] - f0[g] * s0 - f1[g] * s1 for g in groups]
            r0 = spread(rest[home], t)
            r1 = spread(rest[home], t + 1)
            over = 1.0 / a
            at = start + t
            w_ref[at : at + 1, :] = (r0 * lax.rsqrt(a))[:1]
            w_ref[at + 1 : at + 2, :] = ((r1 - (b * over) * r0) * lax.rsqrt(det * over))[:1]
            rest = [rest[g] - f0[g] * r0 - f1[g] * r1 for g in groups]
        after = start + wide
        below = after + wide
        if below < NB:
            pieces = [jnp.zeros((start, NB), F32)] if start else []
            z = jnp.concatenate(pieces + rest + [jnp.zeros((NB - after, NB), F32)], axis=0)
            far = x_ref[below:, :]
            ours = jnp.broadcast_to(mine[:1], far.shape)
            change = dot(jnp.where(ours, far, 0.0), z, ((1,), (0,)))
            x_ref[below:, :] = jnp.where(ours, 0.0, far) - change
        rows = [spread(rest[j // 8], j) for j in range(wide)]
        for h in range(after, min(below, NB), 8):
            x = x_ref[h : h + 8, :]
            terms = [splat(x, start + j) * rows[j] for j in range(wide)]
            while len(terms) > 1:
                terms = [terms[i] + terms[i + 1] for i in range(0, len(terms), 2)]
            x_ref[h : h + 8, :] = jnp.where(mine, 0.0, x) - terms[0]


def indices():
    i = lax.broadcasted_iota(jnp.int32, (NB, NB), 0)
    return i, lax.broadcasted_iota(jnp.int32, (NB, NB), 1)


def pick_body(x, tile, rows, cols):
    first = x[pl.ds(0, NB, stride=4), :]
    odd = (lax.axis_index("row") & 1) == 1
    tile[...] = jnp.where(odd, first.T, first)
    rows[0:NB, :] = first
    rows[NB:, :] = x[pl.ds(4 * NB, NB, stride=4), :]
    for m in range(4):
        cols[NB * m : NB * (m + 1), :] = x[pl.ds(m, NB, stride=4), :]


def token_body(*refs):
    out = refs[-1]
    total = refs[0][...]
    for ref in refs[1:-1]:
        total = total + ref[...]
    out[...] = total


def first_body(mine, other, w0, m10, s11, x):
    even = (lax.axis_index("row") & 1) == 0
    i, j = indices()
    x[...] = jnp.where(even, mine[0:NB, :], other[0:NB, :])
    invert_factor(x, w0)
    w = jnp.where(i >= j, w0[...], 0.0)
    w0[...] = w
    top = jnp.where(even, mine[NB:, :], other[NB:, :])
    bottom = jnp.where(even, other[NB:, :], mine[NB:, :])
    m = dot(w, jnp.concatenate([top, bottom], axis=0), ((1,), (0,)))
    m10[...] = m
    s11[...] = jnp.where(even, other[0:NB, :], mine[0:NB, :]) - dot(m, m, ((0,), (0,)))


def second_body(s11, mark, w1, x):
    i, j = indices()
    x[...] = s11[...]
    invert_factor(x, w1)
    w1[...] = jnp.where(i >= j, w1[...], 0.0)


def finish_body(x, rows_a, rows_b, cols_a, cols_b, w0, m10, w1, out):
    p = lax.axis_index("row")
    q = lax.axis_index("col")
    even = (p & 1) == 0
    direct = (((q + 1) >> 1) & 1) == 0
    i, j = indices()
    low = i >= j
    w0v = w0[...]
    w1v = w1[...]
    m = m10[...]
    r0 = jnp.where(direct, rows_a[...], rows_b[...])
    r1 = jnp.where(direct, rows_b[...], rows_a[...])
    y0 = dot(r0, w0v, ((1,), (1,)))
    y1 = dot(r1 - dot(y0, m, ((1,), (0,))), w1v, ((1,), (1,)))
    y = jnp.concatenate([y0, y1], axis=1)
    for t in range(4):
        at = slice(NB * t, NB * (t + 1))
        ca = cols_a[at, :]
        cb = cols_b[at, :]
        x0 = dot(w0v, jnp.where(even, ca, cb), ((1,), (0,)))
        x1 = dot(w1v, jnp.where(even, cb, ca) - dot(m, x0, ((0,), (0,))), ((1,), (0,)))
        change = dot(y, jnp.concatenate([x0, x1], axis=0), ((1,), (0,)))
        for l in range(2):
            here = pl.ds(4 * NB * l + t, NB, stride=4)
            rs = slice(NB * l, NB * (l + 1))
            new = x[here, :] - change[rs]
            if t == 0:
                panel = jnp.where(q == 0, y0[rs], y1[rs])
                if l == 0:
                    panel = jnp.where((p != q) | low, panel, 0.0)
                    panel = jnp.where((p == 0) & (q == 1), 0.0, panel)
                new = jnp.where(q < 2, panel, new)
                if l == 0:
                    new = jnp.where((p < 2) & (q >= 2), 0.0, new)
            elif l == 0:
                new = jnp.where(p < 2, 0.0, new)
            out[here, :] = new


def tile_of(*rows):
    return [jax.ShapeDtypeStruct((r, NB), F32) for r in rows]


LONG = pl.CostEstimate(flops=COST, bytes_accessed=COST, transcendentals=0)


def call(body, shapes, scratch, *args, cost=None):
    return pl.pallas_call(
        body,
        out_shape=shapes,
        in_specs=[VMEM] * len(args),
        out_specs=[VMEM] * len(shapes),
        scratch_shapes=[pltpu.VMEM((NB, NB), F32)] * scratch,
        compiler_params=PARAMS,
        cost_estimate=cost,
    )(*args)


def token(*xs):
    block = pl.BlockSpec((8, NB), lambda i: (0, 0))
    return pl.pallas_call(
        token_body,
        grid=(1,),
        out_shape=jax.ShapeDtypeStruct((8, NB), F32),
        in_specs=[block] * len(xs),
        out_specs=block,
        compiler_params=PARAMS,
        cost_estimate=LONG,
    )(*xs)


def per_device(covariance):
    p = lax.axis_index("row")
    q = lax.axis_index("col")
    z = p >> 1
    x = q >> 2
    y = q & 3
    odd = (p & 1) == 1
    local = covariance.reshape(2 * NB * 4, NB)
    tile, rows, cols = call(pick_body, tile_of(NB, 2 * NB, 4 * NB), 0, local)

    cores = (0, 1)
    every = range(COLS)
    squares = range(4)
    tied = lax.optimization_barrier

    def in_row(value, pairs):
        return move(value, [((r, a), (r, b)) for r in range(ROWS) for a, b in pairs])

    def along_x(s, d):
        return [(4 * s + a, 4 * d + a) for a in squares]

    def along_z(value, sends, on=cores):
        return move(
            value, [((2 * s + c, a), (2 * d + c, a)) for s, d in sends for c in on for a in every]
        )

    def among(h, members):
        hit = h == members[0]
        for m in members[1:]:
            hit = hit | (h == m)
        return hit

    def take(old, h, got, sends):
        for value, each in zip(got, sends):
            old = jnp.where(among(h, [d for _, d in each]), value, old)
        return old

    swap = [((r, a), (r ^ 1, a)) for r in range(ROWS) for a in every]

    def lift(value, sends):
        return [along_z(value, each) for each in sends]

    r3 = move(tile, [((c, a), (c, b)) for c in cores for a, b in ((0, 1), (1, 0))])
    r1 = move(tile, [((c, a), (c, b)) for c in cores for a, b in ((0, 2), (1, 3))])
    r2 = move(tile, [((c, a), (c, b)) for c in cores for a, b in ((0, 3), (1, 2))])
    for sends in ([(0, 1)], [(1, 5)]):
        cols = take(cols, z, lift(cols, [sends]), [sends])
    c_sends = [[(1, 13), (5, 9)]]
    c_got = lift(cols, c_sends)
    first = jnp.where(y == 0, tile, jnp.where(y == 1, r3, jnp.where(y == 2, r1, r2)))
    second = jnp.where(y == 0, r3, jnp.where(y == 1, tile, jnp.where(y == 2, r2, r1)))
    diag = jnp.concatenate(
        [
            jnp.where(odd, second, first),
            jnp.where(odd, first[NB // 2 :], second[: NB // 2]),
        ],
        axis=0,
    )

    got = [move(diag, [((c, a), (c, b)) for c in cores for a, b in along_x(0, d)]) for d in (2, 1, 3)]
    cols = take(cols, z, c_got, c_sends)
    cols = tied((cols, diag))[0]
    q_sends = [[(1, 2), (5, 4), (13, 12), (9, 8)]]
    q_got = lift(cols, q_sends)
    r_got = in_row(tied((rows, diag))[0], [(0, 3), (1, 2)])
    rows = jnp.where((y >= 2) & (x == 0), r_got, rows)
    far = in_row(tied((rows, diag))[0], along_x(0, 2))
    diag = take(diag, x, got, [[(0, 2)], [(0, 1)], [(0, 3)]])
    diag, mark = tied((diag, token(diag, diag, r_got)))

    d_sends = [[(0, 4)], [(0, 12)], [(0, 2)]]
    got = lift(diag, d_sends)
    rows = jnp.where(x == 2, far, rows)
    r_got = in_row(tied((rows, mark))[0], along_x(0, 1) + along_x(2, 3))
    diag = take(diag, z, got, d_sends)
    diag, mark = tied((diag, token(diag, mark)))

    d_sends = [
        [(0, 13), (2, 5), (4, 8), (12, 9)],
        [(0, 14), (2, 3), (4, 7), (12, 10)],
        [(0, 15), (2, 1), (4, 6), (12, 11)],
    ]
    got = lift(diag, d_sends)
    late_sends = [[(1, 3), (5, 6), (9, 10), (13, 14)], [(5, 7), (9, 11), (13, 15)]]
    late_got = [along_z(tied((cols, mark))[0], each) for each in late_sends]
    diag = take(diag, z, got, d_sends)
    diag, mark = tied((diag, token(diag, mark, *late_got)))

    other = move(diag, swap)
    rows = jnp.where((x & 1) == 1, r_got, rows)
    rows_b = in_row(tied((rows, mark))[0], [(a, a ^ 1) for a in every])
    w0, m10, s11 = call(first_body, tile_of(NB, NB, NB), 1, diag, other)
    cols = take(cols, z, q_got + late_got, q_sends + late_sends)
    cols_b = move(tied((cols, s11))[0], swap)
    (w1,) = call(second_body, tile_of(NB), 1, s11, w0[:8], cost=LONG)
    (out,) = call(
        finish_body, tile_of(8 * NB), 0, local, rows, rows_b, cols, cols_b, w0, m10, w1
    )
    return out.reshape(covariance.shape)


def solution(mesh):
    spec = P(None, "row", None, "col")
    return jax.shard_map(
        per_device, mesh=mesh, in_specs=(spec,), out_specs=spec, check_vma=False
    )
```

```python
import jax
import jax.numpy as jnp
from jax import lax
from jax.experimental import pallas as pl
from jax.experimental.pallas import tpu as pltpu
from jax.sharding import PartitionSpec as P

NB = 128
ROWS = 32
COLS = 16
F32 = jnp.float32
VMEM = pl.BlockSpec(memory_space=pltpu.VMEM)
COST = 10**9
PARAMS = pltpu.CompilerParams(vmem_limit_bytes=8 * 2**20)


def dot(a, b, dims):
    return lax.dot_general(
        a, b, (dims, ((), ())), precision=lax.Precision.HIGHEST, preferred_element_type=F32
    )


def move(value, pairs):
    flat = [(sp * COLS + sq, dp * COLS + dq) for (sp, sq), (dp, dq) in pairs]
    return lax.ppermute(value, ("row", "col"), flat)


def after(value, earlier):
    return lax.optimization_barrier((value, earlier))[0]


def invert_factor(x_ref, w_ref):
    sub = lax.broadcasted_iota(jnp.int32, (8, NB), 0)
    lane = lax.broadcasted_iota(jnp.int32, (8, NB), 1)
    wide = 16
    groups = range(wide // 8)

    def spread(x, j):
        return jnp.broadcast_to(x[j % 8 : j % 8 + 1, :], (8, NB))

    def splat(x, j):
        return jnp.broadcast_to(x[:, j : j + 1], (8, NB))

    for start in range(0, NB, wide):
        here = [x_ref[start + 8 * g : start + 8 * g + 8, :] for g in groups]
        v = [[splat(here[g], start + j) for g in groups] for j in range(wide)]
        mine = (lane >= start) & (lane < start + wide)
        rest = [
            jnp.where(mine, jnp.where(lane == sub + (start + 8 * g), 1.0, 0.0), here[g])
            for g in groups
        ]
        for t in range(0, wide, 2):
            home = t // 8
            u = t % 8
            a = spread(v[t][home], t)
            b = spread(v[t][home], t + 1)
            c = spread(v[t + 1][home], t + 1)
            det = a * c - b * b
            scale = 1.0 / det
            i00 = c * scale
            i01 = b * scale
            i11 = a * scale
            f0 = []
            f1 = []
            for g in groups:
                p0 = v[t][g] * i00 - v[t + 1][g] * i01
                p1 = v[t + 1][g] * i11 - v[t][g] * i01
                if g == home:
                    p0 = jnp.where(sub == u, 1.0 - i00, jnp.where(sub == u + 1, i01, p0))
                    p1 = jnp.where(sub == u, i01, jnp.where(sub == u + 1, 1.0 - i11, p1))
                f0.append(p0)
                f1.append(p1)
            for j in range(t + 2, wide):
                s0 = spread(v[j][home], t)
                s1 = spread(v[j][home], t + 1)
                v[j] = [v[j][g] - f0[g] * s0 - f1[g] * s1 for g in groups]
            r0 = spread(rest[home], t)
            r1 = spread(rest[home], t + 1)
            over = 1.0 / a
            at = start + t
            w_ref[at : at + 1, :] = (r0 * lax.rsqrt(a))[:1]
            w_ref[at + 1 : at + 2, :] = ((r1 - (b * over) * r0) * lax.rsqrt(det * over))[:1]
            rest = [rest[g] - f0[g] * r0 - f1[g] * r1 for g in groups]
        after = start + wide
        below = after + wide
        if below < NB:
            pieces = [jnp.zeros((start, NB), F32)] if start else []
            z = jnp.concatenate(pieces + rest + [jnp.zeros((NB - after, NB), F32)], axis=0)
            far = x_ref[below:, :]
            ours = jnp.broadcast_to(mine[:1], far.shape)
            change = dot(jnp.where(ours, far, 0.0), z, ((1,), (0,)))
            x_ref[below:, :] = jnp.where(ours, 0.0, far) - change
        rows = [spread(rest[j // 8], j) for j in range(wide)]
        for h in range(after, min(below, NB), 8):
            x = x_ref[h : h + 8, :]
            terms = [splat(x, start + j) * rows[j] for j in range(wide)]
            while len(terms) > 1:
                terms = [terms[i] + terms[i + 1] for i in range(0, len(terms), 2)]
            x_ref[h : h + 8, :] = jnp.where(mine, 0.0, x) - terms[0]


def indices():
    i = lax.broadcasted_iota(jnp.int32, (NB, NB), 0)
    return i, lax.broadcasted_iota(jnp.int32, (NB, NB), 1)


def pick_body(x, tile, rows, cols):
    first = x[pl.ds(0, NB, stride=4), :]
    odd = (lax.axis_index("row") & 1) == 1
    tile[...] = jnp.where(odd, first.T, first)
    rows[0:NB, :] = first
    rows[NB:, :] = x[pl.ds(4 * NB, NB, stride=4), :]
    for m in range(4):
        cols[NB * m : NB * (m + 1), :] = x[pl.ds(m, NB, stride=4), :]


def token_body(*refs):
    out = refs[-1]
    total = refs[0][...]
    for ref in refs[1:-1]:
        total = total + ref[...]
    out[...] = total


def first_body(mine, other, w0, m10, s11, x):
    even = (lax.axis_index("row") & 1) == 0
    i, j = indices()
    x[...] = jnp.where(even, mine[0:NB, :], other[0:NB, :])
    invert_factor(x, w0)
    w = jnp.where(i >= j, w0[...], 0.0)
    w0[...] = w
    top = jnp.where(even, mine[NB:, :], other[NB:, :])
    bottom = jnp.where(even, other[NB:, :], mine[NB:, :])
    m = dot(w, jnp.concatenate([top, bottom], axis=0), ((1,), (0,)))
    m10[...] = m
    s11[...] = jnp.where(even, other[0:NB, :], mine[0:NB, :]) - dot(m, m, ((0,), (0,)))


def second_body(s11, mark, w1, x):
    i, j = indices()
    x[...] = s11[...]
    invert_factor(x, w1)
    w1[...] = jnp.where(i >= j, w1[...], 0.0)


def finish_body(x, rows_a, rows_b, cols_a, cols_b, w0, m10, w1, out):
    p = lax.axis_index("row")
    q = lax.axis_index("col")
    even = (p & 1) == 0
    direct = (((q + 1) >> 1) & 1) == 0
    i, j = indices()
    low = i >= j
    w0v = w0[...]
    w1v = w1[...]
    m = m10[...]
    r0 = jnp.where(direct, rows_a[...], rows_b[...])
    r1 = jnp.where(direct, rows_b[...], rows_a[...])
    y0 = dot(r0, w0v, ((1,), (1,)))
    y1 = dot(r1 - dot(y0, m, ((1,), (0,))), w1v, ((1,), (1,)))
    y = jnp.concatenate([y0, y1], axis=1)
    def side(ref):
        return jnp.concatenate([ref[NB * t : NB * (t + 1), :] for t in range(4)], axis=1)

    ca = side(cols_a)
    cb = side(cols_b)
    x0 = dot(w0v, jnp.where(even, ca, cb), ((1,), (0,)))
    x1 = dot(w1v, jnp.where(even, cb, ca) - dot(m, x0, ((0,), (0,))), ((1,), (0,)))
    change = dot(y, jnp.concatenate([x0, x1], axis=0), ((1,), (0,)))
    for t in range(4):
        for l in range(2):
            here = pl.ds(4 * NB * l + t, NB, stride=4)
            rs = slice(NB * l, NB * (l + 1))
            new = x[here, :] - change[rs, NB * t : NB * (t + 1)]
            if t == 0:
                panel = jnp.where(q == 0, y0[rs], y1[rs])
                if l == 0:
                    panel = jnp.where((p != q) | low, panel, 0.0)
                    panel = jnp.where((p == 0) & (q == 1), 0.0, panel)
                new = jnp.where(q < 2, panel, new)
                if l == 0:
                    new = jnp.where((p < 2) & (q >= 2), 0.0, new)
            elif l == 0:
                new = jnp.where(p < 2, 0.0, new)
            out[here, :] = new


def tile_of(*rows):
    return [jax.ShapeDtypeStruct((r, NB), F32) for r in rows]


LONG = pl.CostEstimate(flops=COST, bytes_accessed=COST, transcendentals=0)


def call(body, shapes, scratch, *args, cost=None):
    return pl.pallas_call(
        body,
        out_shape=shapes,
        in_specs=[VMEM] * len(args),
        out_specs=[VMEM] * len(shapes),
        scratch_shapes=[pltpu.VMEM((NB, NB), F32)] * scratch,
        compiler_params=PARAMS,
        cost_estimate=cost,
    )(*args)


def token(*xs):
    block = pl.BlockSpec((8, NB), lambda i: (0, 0))
    return pl.pallas_call(
        token_body,
        grid=(1,),
        out_shape=jax.ShapeDtypeStruct((8, NB), F32),
        in_specs=[block] * len(xs),
        out_specs=block,
        compiler_params=PARAMS,
        cost_estimate=LONG,
    )(*xs)


def per_device(covariance):
    p = lax.axis_index("row")
    q = lax.axis_index("col")
    z = p >> 1
    x = q >> 2
    y = q & 3
    odd = (p & 1) == 1
    local = covariance.reshape(2 * NB * 4, NB)
    tile, rows, cols = call(pick_body, tile_of(NB, 2 * NB, 4 * NB), 0, local)

    cores = (0, 1)
    every = range(COLS)
    squares = range(4)
    tied = lax.optimization_barrier

    def in_row(value, pairs):
        return move(value, [((r, a), (r, b)) for r in range(ROWS) for a, b in pairs])

    def along_x(s, d):
        return [(4 * s + a, 4 * d + a) for a in squares]

    def along_z(value, sends, on=cores):
        return move(
            value, [((2 * s + c, a), (2 * d + c, a)) for s, d in sends for c in on for a in every]
        )

    def among(h, members):
        hit = h == members[0]
        for m in members[1:]:
            hit = hit | (h == m)
        return hit

    def take(old, h, got, sends):
        for value, each in zip(got, sends):
            old = jnp.where(among(h, [d for _, d in each]), value, old)
        return old

    swap = [((r, a), (r ^ 1, a)) for r in range(ROWS) for a in every]

    def lift(value, sends):
        return [along_z(value, each) for each in sends]

    r3 = move(tile, [((c, a), (c, b)) for c in cores for a, b in ((0, 1), (1, 0))])
    r1 = move(tile, [((c, a), (c, b)) for c in cores for a, b in ((0, 2), (1, 3))])
    r2 = move(tile, [((c, a), (c, b)) for c in cores for a, b in ((0, 3), (1, 2))])
    for sends in ([(0, 1)], [(1, 5)]):
        cols = take(cols, z, lift(cols, [sends]), [sends])
    c_sends = [[(1, 13), (5, 9)]]
    c_got = lift(cols, c_sends)
    first = jnp.where(y == 0, tile, jnp.where(y == 1, r3, jnp.where(y == 2, r1, r2)))
    second = jnp.where(y == 0, r3, jnp.where(y == 1, tile, jnp.where(y == 2, r2, r1)))
    diag = jnp.concatenate(
        [
            jnp.where(odd, second, first),
            jnp.where(odd, first[NB // 2 :], second[: NB // 2]),
        ],
        axis=0,
    )

    got = [move(diag, [((c, a), (c, b)) for c in cores for a, b in along_x(0, d)]) for d in (2, 1, 3)]
    cols = take(cols, z, c_got, c_sends)
    cols = tied((cols, diag))[0]
    q_sends = [[(1, 2), (5, 4), (13, 12), (9, 8)]]
    q_got = lift(cols, q_sends)
    r_got = in_row(tied((rows, diag))[0], [(0, 3), (1, 2)])
    rows = jnp.where((y >= 2) & (x == 0), r_got, rows)
    far = in_row(tied((rows, diag))[0], along_x(0, 2))
    diag = take(diag, x, got, [[(0, 2)], [(0, 1)], [(0, 3)]])
    diag, mark = tied((diag, token(diag, diag, r_got)))

    d_sends = [[(0, 4)], [(0, 12)], [(0, 2)]]
    got = lift(diag, d_sends)
    rows = jnp.where(x == 2, far, rows)
    r_got = in_row(tied((rows, mark))[0], along_x(0, 1) + along_x(2, 3))
    diag = take(diag, z, got, d_sends)
    diag, mark = tied((diag, token(diag, mark)))

    d_sends = [
        [(0, 13), (2, 5), (4, 8), (12, 9)],
        [(0, 14), (2, 3), (4, 7), (12, 10)],
        [(0, 15), (2, 1), (4, 6), (12, 11)],
    ]
    got = lift(diag, d_sends)
    late_sends = [[(1, 3), (5, 6), (9, 10), (13, 14)], [(5, 7), (9, 11), (13, 15)]]
    late_got = [along_z(tied((cols, mark))[0], each) for each in late_sends]
    diag = take(diag, z, got, d_sends)
    diag, mark = tied((diag, token(diag, mark, *late_got)))

    other = move(diag, swap)
    rows = jnp.where((x & 1) == 1, r_got, rows)
    rows_b = in_row(tied((rows, mark))[0], [(a, a ^ 1) for a in every])
    w0, m10, s11 = call(first_body, tile_of(NB, NB, NB), 1, diag, other)
    cols = take(cols, z, q_got + late_got, q_sends + late_sends)
    cols_b = move(tied((cols, s11))[0], swap)
    (w1,) = call(second_body, tile_of(NB), 1, s11, w0[:8], cost=LONG)
    (out,) = call(
        finish_body, tile_of(8 * NB), 0, local, rows, rows_b, cols, cols_b, w0, m10, w1
    )
    return out.reshape(covariance.shape)


def solution(mesh):
    spec = P(None, "row", None, "col")
    return jax.shard_map(
        per_device, mesh=mesh, in_specs=(spec,), out_specs=spec, check_vma=False
    )
```

```python
import jax
import jax.numpy as jnp
from jax import lax
from jax.experimental import pallas as pl
from jax.experimental.pallas import tpu as pltpu
from jax.sharding import PartitionSpec as P

NB = 128
ROWS = 32
COLS = 16
F32 = jnp.float32
VMEM = pl.BlockSpec(memory_space=pltpu.VMEM)
COST = 10**9
PARAMS = pltpu.CompilerParams(vmem_limit_bytes=8 * 2**20)


def dot(a, b, dims):
    return lax.dot_general(
        a, b, (dims, ((), ())), precision=lax.Precision.HIGHEST, preferred_element_type=F32
    )


def move(value, pairs):
    flat = [(sp * COLS + sq, dp * COLS + dq) for (sp, sq), (dp, dq) in pairs]
    return lax.ppermute(value, ("row", "col"), flat)


def after(value, earlier):
    return lax.optimization_barrier((value, earlier))[0]


def invert_factor(x_ref, w_ref):
    sub = lax.broadcasted_iota(jnp.int32, (8, NB), 0)
    lane = lax.broadcasted_iota(jnp.int32, (8, NB), 1)
    wide = 16
    groups = range(wide // 8)

    def spread(x, j):
        return jnp.broadcast_to(x[j % 8 : j % 8 + 1, :], (8, NB))

    def splat(x, j):
        return jnp.broadcast_to(x[:, j : j + 1], (8, NB))

    for start in range(0, NB, wide):
        here = [x_ref[start + 8 * g : start + 8 * g + 8, :] for g in groups]
        v = [[splat(here[g], start + j) for g in groups] for j in range(wide)]
        mine = (lane >= start) & (lane < start + wide)
        rest = [
            jnp.where(mine, jnp.where(lane == sub + (start + 8 * g), 1.0, 0.0), here[g])
            for g in groups
        ]
        for t in range(0, wide, 2):
            home = t // 8
            u = t % 8
            a = spread(v[t][home], t)
            b = spread(v[t][home], t + 1)
            c = spread(v[t + 1][home], t + 1)
            det = a * c - b * b
            scale = 1.0 / det
            i00 = c * scale
            i01 = b * scale
            i11 = a * scale
            f0 = []
            f1 = []
            for g in groups:
                p0 = v[t][g] * i00 - v[t + 1][g] * i01
                p1 = v[t + 1][g] * i11 - v[t][g] * i01
                if g == home:
                    p0 = jnp.where(sub == u, 1.0 - i00, jnp.where(sub == u + 1, i01, p0))
                    p1 = jnp.where(sub == u, i01, jnp.where(sub == u + 1, 1.0 - i11, p1))
                f0.append(p0)
                f1.append(p1)
            for j in range(t + 2, wide):
                s0 = spread(v[j][home], t)
                s1 = spread(v[j][home], t + 1)
                v[j] = [v[j][g] - f0[g] * s0 - f1[g] * s1 for g in groups]
            r0 = spread(rest[home], t)
            r1 = spread(rest[home], t + 1)
            over = 1.0 / a
            at = start + t
            w_ref[at : at + 1, :] = (r0 * lax.rsqrt(a))[:1]
            w_ref[at + 1 : at + 2, :] = ((r1 - (b * over) * r0) * lax.rsqrt(det * over))[:1]
            rest = [rest[g] - f0[g] * r0 - f1[g] * r1 for g in groups]
        after = start + wide
        below = after + wide
        if below < NB:
            pieces = [jnp.zeros((start, NB), F32)] if start else []
            z = jnp.concatenate(pieces + rest + [jnp.zeros((NB - after, NB), F32)], axis=0)
            far = x_ref[below:, :]
            ours = jnp.broadcast_to(mine[:1], far.shape)
            change = dot(jnp.where(ours, far, 0.0), z, ((1,), (0,)))
            x_ref[below:, :] = jnp.where(ours, 0.0, far) - change
        rows = [spread(rest[j // 8], j) for j in range(wide)]
        for h in range(after, min(below, NB), 8):
            x = x_ref[h : h + 8, :]
            terms = [splat(x, start + j) * rows[j] for j in range(wide)]
            while len(terms) > 1:
                terms = [terms[i] + terms[i + 1] for i in range(0, len(terms), 2)]
            x_ref[h : h + 8, :] = jnp.where(mine, 0.0, x) - terms[0]


def indices():
    i = lax.broadcasted_iota(jnp.int32, (NB, NB), 0)
    return i, lax.broadcasted_iota(jnp.int32, (NB, NB), 1)


def pick_body(x, tile, rows, cols):
    first = x[pl.ds(0, NB, stride=4), :]
    odd = (lax.axis_index("row") & 1) == 1
    tile[...] = jnp.where(odd, first.T, first)
    rows[0:NB, :] = first
    rows[NB:, :] = x[pl.ds(4 * NB, NB, stride=4), :]
    for m in range(4):
        cols[NB * m : NB * (m + 1), :] = x[pl.ds(m, NB, stride=4), :]


def token_body(*refs):
    out = refs[-1]
    total = refs[0][...]
    for ref in refs[1:-1]:
        total = total + ref[...]
    out[...] = total


def first_body(mine, other, w0, m10, s11, x):
    even = (lax.axis_index("row") & 1) == 0
    i, j = indices()
    x[...] = jnp.where(even, mine[0:NB, :], other[0:NB, :])
    invert_factor(x, w0)
    w = jnp.where(i >= j, w0[...], 0.0)
    w0[...] = w
    top = jnp.where(even, mine[NB:, :], other[NB:, :])
    bottom = jnp.where(even, other[NB:, :], mine[NB:, :])
    m = dot(w, jnp.concatenate([top, bottom], axis=0), ((1,), (0,)))
    m10[...] = m
    s11[...] = jnp.where(even, other[0:NB, :], mine[0:NB, :]) - dot(m, m, ((0,), (0,)))


def second_body(s11, mark, w1, x):
    i, j = indices()
    x[...] = s11[...]
    invert_factor(x, w1)
    w1[...] = jnp.where(i >= j, w1[...], 0.0)


def finish_body(x, rows_a, rows_b, cols_a, cols_b, w0, m10, w1, out):
    p = lax.axis_index("row")
    q = lax.axis_index("col")
    even = (p & 1) == 0
    direct = (((q + 1) >> 1) & 1) == 0
    i, j = indices()
    low = i >= j
    w0v = w0[...]
    w1v = w1[...]
    m = m10[...]
    r0 = jnp.where(direct, rows_a[...], rows_b[...])
    r1 = jnp.where(direct, rows_b[...], rows_a[...])
    y0 = dot(r0, w0v, ((1,), (1,)))
    y1 = dot(r1 - dot(y0, m, ((1,), (0,))), w1v, ((1,), (1,)))
    y = jnp.concatenate([y0, y1], axis=1)
    def side(ref):
        return jnp.concatenate([ref[NB * t : NB * (t + 1), :] for t in range(4)], axis=1)

    ca = side(cols_a)
    cb = side(cols_b)
    x0 = dot(w0v, jnp.where(even, ca, cb), ((1,), (0,)))
    x1 = dot(w1v, jnp.where(even, cb, ca) - dot(m, x0, ((0,), (0,))), ((1,), (0,)))
    change = dot(y, jnp.concatenate([x0, x1], axis=0), ((1,), (0,)))
    for t in range(4):
        for l in range(2):
            here = pl.ds(4 * NB * l + t, NB, stride=4)
            rs = slice(NB * l, NB * (l + 1))
            new = x[here, :] - change[rs, NB * t : NB * (t + 1)]
            if t == 0:
                panel = jnp.where(q == 0, y0[rs], y1[rs])
                if l == 0:
                    panel = jnp.where((p != q) | low, panel, 0.0)
                    panel = jnp.where((p == 0) & (q == 1), 0.0, panel)
                new = jnp.where(q < 2, panel, new)
                if l == 0:
                    new = jnp.where((p < 2) & (q >= 2), 0.0, new)
            elif l == 0:
                new = jnp.where(p < 2, 0.0, new)
            out[here, :] = new


def tile_of(*rows):
    return [jax.ShapeDtypeStruct((r, NB), F32) for r in rows]


LONG = pl.CostEstimate(flops=COST, bytes_accessed=COST, transcendentals=0)


def call(body, shapes, scratch, *args, cost=None):
    return pl.pallas_call(
        body,
        out_shape=shapes,
        in_specs=[VMEM] * len(args),
        out_specs=[VMEM] * len(shapes),
        scratch_shapes=[pltpu.VMEM((NB, NB), F32)] * scratch,
        compiler_params=PARAMS,
        cost_estimate=cost,
    )(*args)


def token(*xs):
    block = pl.BlockSpec((8, NB), lambda i: (0, 0))
    return pl.pallas_call(
        token_body,
        grid=(1,),
        out_shape=jax.ShapeDtypeStruct((8, NB), F32),
        in_specs=[block] * len(xs),
        out_specs=block,
        compiler_params=PARAMS,
        cost_estimate=LONG,
    )(*xs)


def per_device(covariance):
    p = lax.axis_index("row")
    q = lax.axis_index("col")
    z = p >> 1
    x = q >> 2
    y = q & 3
    odd = (p & 1) == 1
    local = covariance.reshape(2 * NB * 4, NB)
    tile, rows, cols = call(pick_body, tile_of(NB, 2 * NB, 4 * NB), 0, local)

    cores = (0, 1)
    every = range(COLS)
    squares = range(4)
    tied = lax.optimization_barrier

    def in_row(value, pairs):
        return move(value, [((r, a), (r, b)) for r in range(ROWS) for a, b in pairs])

    def along_x(s, d):
        return [(4 * s + a, 4 * d + a) for a in squares]

    def along_z(value, sends, on=cores):
        return move(
            value, [((2 * s + c, a), (2 * d + c, a)) for s, d in sends for c in on for a in every]
        )

    def among(h, members):
        hit = h == members[0]
        for m in members[1:]:
            hit = hit | (h == m)
        return hit

    def take(old, h, got, sends):
        for value, each in zip(got, sends):
            old = jnp.where(among(h, [d for _, d in each]), value, old)
        return old

    swap = [((r, a), (r ^ 1, a)) for r in range(ROWS) for a in every]

    def lift(value, sends):
        return [along_z(value, each) for each in sends]

    r3 = move(tile, [((c, a), (c, b)) for c in cores for a, b in ((0, 1), (1, 0))])
    r2 = move(tile, [((c, a), (c, b)) for c in cores for a, b in ((0, 3), (1, 2))])
    r1 = move(tile, [((c, a), (c, b)) for c in cores for a, b in ((0, 2), (1, 3))])
    for sends in ([(0, 1)], [(1, 5)]):
        cols = take(cols, z, lift(cols, [sends]), [sends])
    c_sends = [[(1, 13), (5, 9)]]
    c_got = lift(cols, c_sends)
    first = jnp.where(y == 0, tile, jnp.where(y == 1, r3, jnp.where(y == 2, r1, r2)))
    second = jnp.where(y == 0, r3, jnp.where(y == 1, tile, jnp.where(y == 2, r2, r1)))
    diag = jnp.concatenate(
        [
            jnp.where(odd, second, first),
            jnp.where(odd, first[NB // 2 :], second[: NB // 2]),
        ],
        axis=0,
    )

    got = [move(diag, [((c, a), (c, b)) for c in cores for a, b in along_x(0, d)]) for d in (3, 1, 2)]
    cols = take(cols, z, c_got, c_sends)
    cols = tied((cols, diag))[0]
    q_sends = [[(1, 2), (5, 4), (13, 12), (9, 8)]]
    q_got = lift(cols, q_sends)
    r_got = in_row(tied((rows, diag))[0], [(0, 3), (1, 2)])
    rows = jnp.where((y >= 2) & (x == 0), r_got, rows)
    far = in_row(tied((rows, diag))[0], along_x(0, 2))
    diag = take(diag, x, got, [[(0, 3)], [(0, 1)], [(0, 2)]])
    diag, mark = tied((diag, token(diag, diag, r_got)))

    d_sends = [[(0, 4)], [(0, 2)], [(0, 12)]]
    got = lift(diag, d_sends)
    rows = jnp.where(x == 2, far, rows)
    r_got = in_row(tied((rows, mark))[0], along_x(0, 1) + along_x(2, 3))
    diag = take(diag, z, got, d_sends)
    diag, mark = tied((diag, token(diag, mark)))

    d_sends = [
        [(0, 13), (2, 5), (4, 8), (12, 9)],
        [(0, 15), (2, 1), (4, 6), (12, 11)],
        [(0, 14), (2, 3), (4, 7), (12, 10)],
    ]
    got = lift(diag, d_sends)
    late_sends = [[(5, 7), (9, 11), (13, 15)], [(1, 3), (5, 6), (9, 10), (13, 14)]]
    late_got = [along_z(tied((cols, mark))[0], each) for each in late_sends]
    diag = take(diag, z, got, d_sends)
    diag, mark = tied((diag, token(diag, mark, *late_got)))

    other = move(diag, swap)
    rows = jnp.where((x & 1) == 1, r_got, rows)
    rows_b = in_row(tied((rows, mark))[0], [(a, a ^ 1) for a in every])
    w0, m10, s11 = call(first_body, tile_of(NB, NB, NB), 1, diag, other)
    cols = take(cols, z, q_got + late_got, q_sends + late_sends)
    cols_b = move(tied((cols, s11))[0], swap)
    (w1,) = call(second_body, tile_of(NB), 1, s11, w0[:8], cost=LONG)
    (out,) = call(
        finish_body, tile_of(8 * NB), 0, local, rows, rows_b, cols, cols_b, w0, m10, w1
    )
    return out.reshape(covariance.shape)


def solution(mesh):
    spec = P(None, "row", None, "col")
    return jax.shard_map(
        per_device, mesh=mesh, in_specs=(spec,), out_specs=spec, check_vma=False
    )
```

```python
import jax
import jax.numpy as jnp
from jax import lax
from jax.experimental import pallas as pl
from jax.experimental.pallas import tpu as pltpu
from jax.sharding import PartitionSpec as P

NB = 128
ROWS = 32
COLS = 16
F32 = jnp.float32
VMEM = pl.BlockSpec(memory_space=pltpu.VMEM)
COST = 10**9
PARAMS = pltpu.CompilerParams(vmem_limit_bytes=8 * 2**20)


def dot(a, b, dims):
    return lax.dot_general(
        a, b, (dims, ((), ())), precision=lax.Precision.HIGHEST, preferred_element_type=F32
    )


def move(value, pairs):
    flat = [(sp * COLS + sq, dp * COLS + dq) for (sp, sq), (dp, dq) in pairs]
    return lax.ppermute(value, ("row", "col"), flat)


def after(value, earlier):
    return lax.optimization_barrier((value, earlier))[0]


def invert_factor(x_ref, w_ref):
    sub = lax.broadcasted_iota(jnp.int32, (8, NB), 0)
    lane = lax.broadcasted_iota(jnp.int32, (8, NB), 1)
    wide = 16
    groups = range(wide // 8)

    def spread(x, j):
        return jnp.broadcast_to(x[j % 8 : j % 8 + 1, :], (8, NB))

    def splat(x, j):
        return jnp.broadcast_to(x[:, j : j + 1], (8, NB))

    for start in range(0, NB, wide):
        here = [x_ref[start + 8 * g : start + 8 * g + 8, :] for g in groups]
        v = [[splat(here[g], start + j) for g in groups] for j in range(wide)]
        mine = (lane >= start) & (lane < start + wide)
        rest = [
            jnp.where(mine, jnp.where(lane == sub + (start + 8 * g), 1.0, 0.0), here[g])
            for g in groups
        ]
        for t in range(0, wide, 2):
            home = t // 8
            u = t % 8
            a = spread(v[t][home], t)
            b = spread(v[t][home], t + 1)
            c = spread(v[t + 1][home], t + 1)
            det = a * c - b * b
            scale = 1.0 / det
            i00 = c * scale
            i01 = b * scale
            i11 = a * scale
            f0 = []
            f1 = []
            for g in groups:
                p0 = v[t][g] * i00 - v[t + 1][g] * i01
                p1 = v[t + 1][g] * i11 - v[t][g] * i01
                if g == home:
                    p0 = jnp.where(sub == u, 1.0 - i00, jnp.where(sub == u + 1, i01, p0))
                    p1 = jnp.where(sub == u, i01, jnp.where(sub == u + 1, 1.0 - i11, p1))
                f0.append(p0)
                f1.append(p1)
            for j in range(t + 2, wide):
                s0 = spread(v[j][home], t)
                s1 = spread(v[j][home], t + 1)
                v[j] = [v[j][g] - f0[g] * s0 - f1[g] * s1 for g in groups]
            r0 = spread(rest[home], t)
            r1 = spread(rest[home], t + 1)
            over = 1.0 / a
            at = start + t
            w_ref[at : at + 1, :] = (r0 * lax.rsqrt(a))[:1]
            w_ref[at + 1 : at + 2, :] = ((r1 - (b * over) * r0) * lax.rsqrt(det * over))[:1]
            rest = [rest[g] - f0[g] * r0 - f1[g] * r1 for g in groups]
        after = start + wide
        below = after + wide
        if below < NB:
            pieces = [jnp.zeros((start, NB), F32)] if start else []
            z = jnp.concatenate(pieces + rest + [jnp.zeros((NB - after, NB), F32)], axis=0)
            far = x_ref[below:, :]
            ours = jnp.broadcast_to(mine[:1], far.shape)
            change = dot(jnp.where(ours, far, 0.0), z, ((1,), (0,)))
            x_ref[below:, :] = jnp.where(ours, 0.0, far) - change
        rows = [spread(rest[j // 8], j) for j in range(wide)]
        for h in range(after, min(below, NB), 8):
            x = x_ref[h : h + 8, :]
            terms = [splat(x, start + j) * rows[j] for j in range(wide)]
            while len(terms) > 1:
                terms = [terms[i] + terms[i + 1] for i in range(0, len(terms), 2)]
            x_ref[h : h + 8, :] = jnp.where(mine, 0.0, x) - terms[0]


def indices():
    i = lax.broadcasted_iota(jnp.int32, (NB, NB), 0)
    return i, lax.broadcasted_iota(jnp.int32, (NB, NB), 1)


def corner_body(x, tile):
    first = x[pl.ds(0, NB, stride=4), :]
    odd = (lax.axis_index("row") & 1) == 1
    tile[...] = jnp.where(odd, first.T, first)


def pick_body(x, rows, cols):
    rows[0:NB, :] = x[pl.ds(0, NB, stride=4), :]
    rows[NB:, :] = x[pl.ds(4 * NB, NB, stride=4), :]
    for m in range(4):
        cols[NB * m : NB * (m + 1), :] = x[pl.ds(m, NB, stride=4), :]


def token_body(*refs):
    out = refs[-1]
    total = refs[0][...]
    for ref in refs[1:-1]:
        total = total + ref[...]
    out[...] = total


def first_body(mine, other, w0, m10, s11, x):
    even = (lax.axis_index("row") & 1) == 0
    i, j = indices()
    x[...] = jnp.where(even, mine[0:NB, :], other[0:NB, :])
    invert_factor(x, w0)
    w = jnp.where(i >= j, w0[...], 0.0)
    w0[...] = w
    top = jnp.where(even, mine[NB:, :], other[NB:, :])
    bottom = jnp.where(even, other[NB:, :], mine[NB:, :])
    m = dot(w, jnp.concatenate([top, bottom], axis=0), ((1,), (0,)))
    m10[...] = m
    s11[...] = jnp.where(even, other[0:NB, :], mine[0:NB, :]) - dot(m, m, ((0,), (0,)))


def second_body(s11, mark, w1, x):
    i, j = indices()
    x[...] = s11[...]
    invert_factor(x, w1)
    w1[...] = jnp.where(i >= j, w1[...], 0.0)


def finish_body(x, rows_a, rows_b, cols_a, cols_b, w0, m10, w1, out):
    p = lax.axis_index("row")
    q = lax.axis_index("col")
    even = (p & 1) == 0
    direct = (((q + 1) >> 1) & 1) == 0
    i, j = indices()
    low = i >= j
    w0v = w0[...]
    w1v = w1[...]
    m = m10[...]
    r0 = jnp.where(direct, rows_a[...], rows_b[...])
    r1 = jnp.where(direct, rows_b[...], rows_a[...])
    y0 = dot(r0, w0v, ((1,), (1,)))
    y1 = dot(r1 - dot(y0, m, ((1,), (0,))), w1v, ((1,), (1,)))
    y = jnp.concatenate([y0, y1], axis=1)
    def side(ref):
        return jnp.concatenate([ref[NB * t : NB * (t + 1), :] for t in range(4)], axis=1)

    ca = side(cols_a)
    cb = side(cols_b)
    x0 = dot(w0v, jnp.where(even, ca, cb), ((1,), (0,)))
    x1 = dot(w1v, jnp.where(even, cb, ca) - dot(m, x0, ((0,), (0,))), ((1,), (0,)))
    change = dot(y, jnp.concatenate([x0, x1], axis=0), ((1,), (0,)))
    for t in range(4):
        for l in range(2):
            here = pl.ds(4 * NB * l + t, NB, stride=4)
            rs = slice(NB * l, NB * (l + 1))
            new = x[here, :] - change[rs, NB * t : NB * (t + 1)]
            if t == 0:
                panel = jnp.where(q == 0, y0[rs], y1[rs])
                if l == 0:
                    panel = jnp.where((p != q) | low, panel, 0.0)
                    panel = jnp.where((p == 0) & (q == 1), 0.0, panel)
                new = jnp.where(q < 2, panel, new)
                if l == 0:
                    new = jnp.where((p < 2) & (q >= 2), 0.0, new)
            elif l == 0:
                new = jnp.where(p < 2, 0.0, new)
            out[here, :] = new


def tile_of(*rows):
    return [jax.ShapeDtypeStruct((r, NB), F32) for r in rows]


LONG = pl.CostEstimate(flops=COST, bytes_accessed=COST, transcendentals=0)


def call(body, shapes, scratch, *args, cost=None):
    return pl.pallas_call(
        body,
        out_shape=shapes,
        in_specs=[VMEM] * len(args),
        out_specs=[VMEM] * len(shapes),
        scratch_shapes=[pltpu.VMEM((NB, NB), F32)] * scratch,
        compiler_params=PARAMS,
        cost_estimate=cost,
    )(*args)


def token(*xs):
    block = pl.BlockSpec((8, NB), lambda i: (0, 0))
    return pl.pallas_call(
        token_body,
        grid=(1,),
        out_shape=jax.ShapeDtypeStruct((8, NB), F32),
        in_specs=[block] * len(xs),
        out_specs=block,
        compiler_params=PARAMS,
        cost_estimate=LONG,
    )(*xs)


def per_device(covariance):
    p = lax.axis_index("row")
    q = lax.axis_index("col")
    z = p >> 1
    x = q >> 2
    y = q & 3
    odd = (p & 1) == 1
    local = covariance.reshape(2 * NB * 4, NB)
    tile = pl.pallas_call(
        corner_body,
        grid=(1,),
        out_shape=tile_of(NB)[0],
        in_specs=[pl.BlockSpec((4 * NB, NB), lambda i: (0, 0))],
        out_specs=pl.BlockSpec((NB, NB), lambda i: (0, 0)),
        compiler_params=PARAMS,
    )(local[: 4 * NB])
    rows, cols = call(pick_body, tile_of(2 * NB, 4 * NB), 0, local)

    cores = (0, 1)
    every = range(COLS)
    squares = range(4)
    tied = lax.optimization_barrier

    def in_row(value, pairs):
        return move(value, [((r, a), (r, b)) for r in range(ROWS) for a, b in pairs])

    def along_x(s, d):
        return [(4 * s + a, 4 * d + a) for a in squares]

    def along_z(value, sends, on=cores):
        return move(
            value, [((2 * s + c, a), (2 * d + c, a)) for s, d in sends for c in on for a in every]
        )

    def among(h, members):
        hit = h == members[0]
        for m in members[1:]:
            hit = hit | (h == m)
        return hit

    def take(old, h, got, sends):
        for value, each in zip(got, sends):
            old = jnp.where(among(h, [d for _, d in each]), value, old)
        return old

    swap = [((r, a), (r ^ 1, a)) for r in range(ROWS) for a in every]

    def lift(value, sends):
        return [along_z(value, each) for each in sends]

    r3 = move(tile, [((c, a), (c, b)) for c in cores for a, b in ((0, 1), (1, 0))])
    r1 = move(tile, [((c, a), (c, b)) for c in cores for a, b in ((0, 2), (1, 3))])
    r2 = move(tile, [((c, a), (c, b)) for c in cores for a, b in ((0, 3), (1, 2))])
    for sends in ([(0, 1)], [(1, 5)]):
        cols = take(cols, z, lift(cols, [sends]), [sends])
    c_sends = [[(1, 13), (5, 9)]]
    c_got = lift(cols, c_sends)
    first = jnp.where(y == 0, tile, jnp.where(y == 1, r3, jnp.where(y == 2, r1, r2)))
    second = jnp.where(y == 0, r3, jnp.where(y == 1, tile, jnp.where(y == 2, r2, r1)))
    diag = jnp.concatenate(
        [
            jnp.where(odd, second, first),
            jnp.where(odd, first[NB // 2 :], second[: NB // 2]),
        ],
        axis=0,
    )

    got = [move(diag, [((c, a), (c, b)) for c in cores for a, b in along_x(0, d)]) for d in (2, 1, 3)]
    cols = take(cols, z, c_got, c_sends)
    cols = tied((cols, diag))[0]
    q_sends = [[(1, 2), (5, 4), (13, 12), (9, 8)]]
    q_got = lift(cols, q_sends)
    r_got = in_row(tied((rows, diag))[0], [(0, 3), (1, 2)])
    rows = jnp.where((y >= 2) & (x == 0), r_got, rows)
    far = in_row(tied((rows, diag))[0], along_x(0, 2))
    diag = take(diag, x, got, [[(0, 2)], [(0, 1)], [(0, 3)]])
    diag, mark = tied((diag, token(diag, diag, r_got)))

    d_sends = [[(0, 4)], [(0, 12)], [(0, 2)]]
    got = lift(diag, d_sends)
    rows = jnp.where(x == 2, far, rows)
    r_got = in_row(tied((rows, mark))[0], along_x(0, 1) + along_x(2, 3))
    diag = take(diag, z, got, d_sends)
    diag, mark = tied((diag, token(diag, mark)))

    d_sends = [
        [(0, 13), (2, 5), (4, 8), (12, 9)],
        [(0, 14), (2, 3), (4, 7), (12, 10)],
        [(0, 15), (2, 1), (4, 6), (12, 11)],
    ]
    got = lift(diag, d_sends)
    late_sends = [[(1, 3), (5, 6), (9, 10), (13, 14)], [(5, 7), (9, 11), (13, 15)]]
    late_got = [along_z(tied((cols, mark))[0], each) for each in late_sends]
    diag = take(diag, z, got, d_sends)
    diag, mark = tied((diag, token(diag, mark, *late_got)))

    other = move(diag, swap)
    rows = jnp.where((x & 1) == 1, r_got, rows)
    rows_b = in_row(tied((rows, mark))[0], [(a, a ^ 1) for a in every])
    w0, m10, s11 = call(first_body, tile_of(NB, NB, NB), 1, diag, other)
    cols = take(cols, z, q_got + late_got, q_sends + late_sends)
    cols_b = move(tied((cols, s11))[0], swap)
    (w1,) = call(second_body, tile_of(NB), 1, s11, w0[:8], cost=LONG)
    (out,) = call(
        finish_body, tile_of(8 * NB), 0, local, rows, rows_b, cols, cols_b, w0, m10, w1
    )
    return out.reshape(covariance.shape)


def solution(mesh):
    spec = P(None, "row", None, "col")
    return jax.shard_map(
        per_device, mesh=mesh, in_specs=(spec,), out_specs=spec, check_vma=False
    )
```
